32 devices in a mesh: req: 4 (over z), wide: 8 (over y, x, core).
Axes of the slice: x: 2, y: 2, z: 4, core: 2. Of those that a mesh axis runs over, the one named last changes fastest.
Arguments:
- queries: bfloat16 [4096, 3072], P(('req', 'wide'))
- suffix_latent: bfloat16 [4096, 512], P(('req', 'wide')), may hold values from -6 to 6
- suffix_rope: bfloat16 [64, 4096], P(None, ('req', 'wide')), may hold values from -6 to 6
- residual: bfloat16 [4096, 2048], P(('req', 'wide')), may hold values from -3 to 3
- prefix_latent: bfloat16 [4, 2, 1024, 512], P('req', None, 'wide'), may hold values from -6 to 6
- prefix_rope: bfloat16 [4, 2, 64, 1024], P('req', None, None, 'wide')
- suffix_lengths: int32 [32, 4], P(('req', 'wide')), may hold values from 1 to 64, 128 in all within a row
- prefix_ids: int32 [32, 4], P(('req', 'wide')), may hold values from 0 to 1
- w_ukv: bfloat16 [512, 4096], replicated, may hold values from -0.25 to 0.25
- w_out: bfloat16 [2048, 2048], replicated, may hold values from -0.5 to 0.5
- norm_gain: bfloat16 [2048], replicated, may hold values from 0.099609375 to 1.8984375
- expert_ids: int32 [4096, 6], P(('req', 'wide')), may hold values from 0 to 15, all different within a row; in each aligned block of 128 rows (0 to 127, 128 to 255, ...) at most 49 rows name the same one
- gate_values: float32 [4096, 6], P(('req', 'wide')), may hold values from 0.05 to 0.45
- expert_gate_up: bfloat16 [32, 2048, 1408], P(('req', 'wide')), may hold values from -0.125 to 0.125
- expert_down: bfloat16 [32, 704, 2048], P(('req', 'wide')), may hold values from -0.15625 to 0.15625
Outputs:
- layer_out: bfloat16 [4096, 2048], P(('req', 'wide'))
The draws below stay inside these ranges and needn't reach their ends.
Inputs may be any that keep to these rules, and one draw needn't show every extreme that they name: `suffix_lengths`: row b gives, in order, the lengths of the 4 requests that make up tokens b * 128 to (b + 1) * 128 - 1; each row sums to 128 and its largest entry is 64. `expert_ids`: a token's 6 experts differ; among the 128 tokens of one device no expert is named more than 49 times, and in some device one expert is named exactly 49 times.
All inputs are finite; a program needn't handle non-finite values.
Results may differ from the reference program's by a relative error of at most 0.012.
Values may be sent and summed in bfloat16 or wider, within the bound.
A program may use at most 192 MiB of HBM per device.

```python
import math
import jax
import jax.numpy as jnp
import numpy as np
from jax import lax

D = 2048
HEADS = 16
NOPE = 128
ROPE = 64
LAT = 512
FF_E = 1408
TOP = 6
PREF = 2
REQ_DEV = 4
TOK_DEV = 128
PLEN_DEV = 128
GROUPS = 4
EXPERTS = 16
TOKENS = 4096
PLEN = 1024
CAP = 49
N_WIDE = 8
DEVICES = 32


def draw_queries(key, part):
    row_width = HEADS * (NOPE + ROPE)
    return (2.0 * jax.random.truncated_normal(jax.random.fold_in(key, 1), -6.0, 6.0, (TOKENS, row_width), jnp.float32)).astype(jnp.bfloat16)


def draw_prefix_rope(key, part):
    array_shape = (GROUPS, PREF, ROPE, PLEN)
    return jax.random.truncated_normal(jax.random.fold_in(key, 2), -6.0, 6.0, array_shape, jnp.float32).astype(jnp.bfloat16)


def touch_ends(result, stream_key, least, high):
    place = [jax.random.randint(jax.random.fold_in(stream_key, axis), (), 0, length) for axis, length in enumerate(result.shape)]
    main_axis = result.shape.index(max(result.shape))
    neighbour = place[:main_axis] + [(place[main_axis] + 1) % result.shape[main_axis]] + place[main_axis + 1:]
    return result.at[tuple(place)].set(least).at[tuple(neighbour)].set(high)


def level_of(own_key, extent, pieces, least, high):
    def one(dim, shards_of):
        draws = jax.random.uniform(jax.random.fold_in(jax.random.fold_in(own_key, 6), dim), (shards_of,), jnp.float32, least / len(pieces), high / len(pieces))
        return jnp.repeat(jnp.exp(draws), extent[dim] // shards_of).reshape((-1,) + (1,) * (len(extent) - dim - 1))

    factor_of = one(*pieces[0])
    for cut in pieces[1:]:
        factor_of = factor_of * one(*cut)
    return factor_of


def length_profile(number_of, total, most, slope):
    loads = [(1 << 20) // math.isqrt(standing ** slope) + 1 for standing in range(2, number_of + 1)]
    rest, given = total - most - (number_of - 1), [1] * (number_of - 1)
    while rest > 0:
        free = [i for i in range(number_of - 1) if given[i] < most]
        pool, budget = sum([loads[i] for i in free]), rest
        for i in free:
            extra = min(most - given[i], max(1, budget * loads[i] // pool), rest)
            given[i] = given[i] + extra
            rest = rest - extra
    return np.array([most] + given)


def ragged(rng, number_of, total, reach, lean):
    if number_of == 2:
        one = jax.random.randint(rng, (), max(1, total - reach), min(reach, total - 1) + 1)
        return jnp.stack([one, total - one])
    tallies = jnp.asarray(length_profile(number_of, total, reach, lean), jnp.int32)
    couples = (number_of - 1) // 2
    giver, sink = tallies[1:1 + 2 * couples:2], tallies[2:2 + 2 * couples:2]
    room = jnp.minimum(giver - 1, reach - sink)
    moved = jax.random.randint(jax.random.fold_in(rng, 1), (couples,), 0, 1 << 20) % (room + 1)
    tallies = tallies.at[1:1 + 2 * couples:2].set(giver - moved).at[2:2 + 2 * couples:2].set(sink + moved)
    return tallies[jax.random.permutation(jax.random.fold_in(rng, 2), number_of)]


def assign_block(key, own, number, rows, count, top, bound, lean):
    order = jax.random.permutation(key, count)
    packed, common = shares(count, rows * top, bound, lean, True), shares(count, rows * top, bound, lean, False)
    places = jnp.arange(count)

    def named(sizes, rotation):
        used = int((sizes > 0).sum())
        fixed = max(1, used // 4)
        shifted = fixed + (places - fixed + rotation * (used - fixed)) % max(1, count - fixed)
        return jnp.zeros((count,), jnp.int32).at[order[jnp.where(places < fixed, places, shifted)]].set(jnp.asarray(sizes, jnp.int32))

    sizes = jnp.where(number % 4 == 0, named(packed, number // 4), named(common, number - number // 4 - 1))
    mixed = jax.random.permutation(jax.random.fold_in(own, 3), count)
    donor, receiver = mixed[0:count // 2 * 2:2], mixed[1:count // 2 * 2:2]
    margin = jnp.minimum(sizes[donor] - 1, bound - sizes[receiver]) // 2
    margin = jnp.where((donor == order[0]) | (receiver == order[0]) | (sizes[receiver] == 0), 0, jnp.maximum(margin, 0))
    shifted = jax.random.randint(jax.random.fold_in(own, 4), (count // 2,), 0, 1 << 20) % (margin + 1)
    sizes = sizes.at[donor].add(-shifted).at[receiver].add(shifted)
    members = jnp.searchsorted(jnp.cumsum(sizes), jnp.arange(rows * top), side="right").astype(jnp.int32)
    grid = members.reshape(top, rows).T
    grid = grid[jax.random.permutation(jax.random.fold_in(own, 1), rows)]
    rotation = jax.random.randint(jax.random.fold_in(own, 2), (rows, 1), 0, top)
    return jnp.take_along_axis(grid, (jnp.arange(top)[None, :] + rotation) % top, axis=1)


def shares(number_of, total, limit, slope, full):
    weights = [(1 << 20) // math.isqrt(grade ** slope) + 1 for grade in range(1, number_of + 1)]
    largest = limit if full else min(limit, max(-(-total // number_of), total * weights[0] // sum(weights)))
    least = 1 if total - largest >= number_of - 1 else 0
    given, rest = [largest] + [least] * (number_of - 1), total - largest - least * (number_of - 1)
    while rest > 0:
        candidates = [i for i in range(1, number_of) if given[i] < largest] or [i for i in range(1, number_of) if given[i] < limit]
        whole, budget = sum([weights[i] for i in candidates]), rest
        for i in candidates:
            extra = min(limit - given[i], max(1, budget * weights[i] // whole), rest)
            given[i] = given[i] + extra
            rest = rest - extra
    return np.array(given)


def bell_draw(stream_key, dims, scale, reach, pieces=(), kind=jnp.bfloat16):
    entries = scale * jax.random.normal(stream_key, dims, jnp.float32)
    if pieces:
        entries = entries * level_of(stream_key, dims, pieces, -0.22, 0.18)
    return jnp.clip(entries, -reach, reach).astype(kind)


def setup_inputs(seed: int = 0) -> dict:
    splits = jax.random.split(jax.random.key(seed), 16)
    queries = draw_queries(jax.random.fold_in(splits[15], 71), 0)
    suffix_latent = bell_draw(splits[1], (TOKENS, LAT), 1.0, 6.0, ((0, 32),))
    suffix_rope = bell_draw(splits[2], (ROPE, TOKENS), 1.0, 6.0, ((1, 32),))
    residual = bell_draw(splits[3], (TOKENS, D), 0.5, 3.0, ((0, 32),))
    prefix_latent = bell_draw(splits[4], (GROUPS, PREF, PLEN, LAT), 1.0, 6.0, ((0, 4), (2, 8)))
    prefix_rope = draw_prefix_rope(jax.random.fold_in(splits[15], 71), 0)
    suffix_lengths = jax.vmap(lambda own: ragged(own, REQ_DEV, TOK_DEV, TOK_DEV // 2, 2))(jax.random.split(splits[6], DEVICES)).reshape((DEVICES, REQ_DEV)).astype(jnp.int32)
    prefix_ids = touch_ends(jax.random.randint(splits[7], (DEVICES, REQ_DEV), 0, PREF), jax.random.fold_in(splits[7], 1), 0, PREF - 1).astype(jnp.int32)
    w_ukv = bell_draw(splits[8], (LAT, HEADS * 2 * NOPE), LAT ** -0.5, 0.25)
    w_out = bell_draw(splits[9], (HEADS * NOPE, D), (HEADS * NOPE // 16) ** -0.5, 0.5)
    norm_gain = jnp.clip(1.0 + 0.18 * jax.random.normal(splits[10], (D,), jnp.float32), 0.099609375, 1.8984375).astype(jnp.bfloat16)
    expert_ids_keys = jax.random.split(jax.random.fold_in(splits[11], 1), TOKENS // TOK_DEV)
    expert_ids_turns = jax.random.permutation(jax.random.fold_in(splits[11], 3), TOKENS // TOK_DEV)
    expert_ids = jax.vmap(lambda own, number: assign_block(jax.random.fold_in(splits[11], 2), own, number, TOK_DEV, EXPERTS, TOP, CAP, 1))(expert_ids_keys, expert_ids_turns).reshape((TOKENS, TOP))
    gate_values = jnp.clip(0.05 + 0.39999999 * jax.random.uniform(splits[12], (TOKENS, TOP), jnp.float32) ** level_of(splits[12], (TOKENS, TOP), ((0, 32),), -0.2, 0.2), 0.05, 0.45)
    expert_gate_up = bell_draw(splits[13], (2 * EXPERTS, D, FF_E), D ** -0.5, 0.125, ((0, 32),))
    expert_down = bell_draw(splits[14], (2 * EXPERTS, FF_E // 2, D), FF_E ** -0.5, 0.15625, ((0, 32),))
    return dict(queries=queries, suffix_latent=suffix_latent, suffix_rope=suffix_rope, residual=residual, prefix_latent=prefix_latent, prefix_rope=prefix_rope, suffix_lengths=suffix_lengths, prefix_ids=prefix_ids, w_ukv=w_ukv, w_out=w_out, norm_gain=norm_gain, expert_ids=expert_ids, gate_values=gate_values, expert_gate_up=expert_gate_up, expert_down=expert_down)


epsilon = 1e-06

def round_trip(values):
    return lax.optimization_barrier(values.astype(jnp.bfloat16)).astype(jnp.float32)

def request_tables(lengths, request_ids):
    request_end = jnp.cumsum(lengths).astype(jnp.int32)
    positions = jnp.arange(TOK_DEV, dtype=jnp.int32)
    segment = lax.optimization_barrier(jnp.sum((positions[:, None] >= request_end[None, :]).astype(jnp.int32), axis=1)).astype(jnp.int32)
    matches = segment[:, None] == jnp.arange(REQ_DEV, dtype=jnp.int32)[None, :]
    prefix = lax.optimization_barrier(jnp.sum(jnp.where(matches, request_ids[None, :], 0), axis=1)).astype(jnp.int32)
    return (segment, prefix)

def project_latent(latent, w_ukv):
    row_count = latent.shape[0]
    joined = jnp.dot(latent, w_ukv, preferred_element_type=jnp.float32).astype(jnp.bfloat16)
    joined = joined.reshape(row_count, HEADS, 2 * NOPE)
    return (joined[:, :, :NOPE], joined[:, :, NOPE:])

def reference(queries, suffix_latent, suffix_rope, residual, prefix_latent, prefix_rope, suffix_lengths, prefix_ids, w_ukv, w_out, norm_gain, expert_ids, gate_values, expert_gate_up, expert_down):
    scaling = 1.0 / (NOPE + ROPE) ** 0.5
    highest = lax.Precision.HIGHEST
    query_all = queries.reshape(GROUPS, N_WIDE, TOK_DEV, HEADS * (NOPE + ROPE))
    latent_all = suffix_latent.reshape(GROUPS, N_WIDE, TOK_DEV, LAT)
    turn_all = suffix_rope.reshape(ROPE, GROUPS, N_WIDE, TOK_DEV).transpose(1, 2, 0, 3)
    residual_all = residual.reshape(GROUPS, N_WIDE, TOK_DEV, D)
    length_all = suffix_lengths.reshape(GROUPS, N_WIDE, REQ_DEV)
    ident_all = prefix_ids.reshape(GROUPS, N_WIDE, REQ_DEV)
    out_heads = w_out.reshape(HEADS, NOPE, D).astype(jnp.float32)
    gain_f32 = norm_gain.astype(jnp.float32)

    def one_group(group_operands):
        query_g, latent_g, turn_g, residual_g, length_g, ident_g, cached_latent, cached_turn = group_operands
        prefix_keys, prefix_values = project_latent(cached_latent.reshape(PREF * PLEN, LAT), w_ukv)
        prefix_keys = prefix_keys.astype(jnp.float32).reshape(PREF, PLEN, HEADS, NOPE)
        prefix_values = prefix_values.astype(jnp.float32).reshape(PREF, N_WIDE, PLEN_DEV, HEADS, NOPE)
        prefix_turn = cached_turn.astype(jnp.float32)

        def one_block(block_operands):
            query_rows, latent_rows, suffix_turn, residual_rows, lengths, request_ids = block_operands
            segment, prefix = request_tables(lengths, request_ids)
            query_f32 = query_rows.astype(jnp.float32)
            query_nope = query_f32[:, :HEADS * NOPE].reshape(TOK_DEV, HEADS, NOPE)
            query_rope = query_f32[:, HEADS * NOPE:].reshape(TOK_DEV, HEADS, ROPE)
            scores = jnp.einsum('thn,pkhn->thpk', query_nope, prefix_keys, precision=highest)
            scores = scores + jnp.einsum('thr,prk->thpk', query_rope, prefix_turn, precision=highest)
            scores = (scores * scaling).reshape(TOK_DEV, HEADS, PREF, N_WIDE, PLEN_DEV)
            own_rows = (prefix[:, None] == jnp.arange(PREF, dtype=jnp.int32)[None, :])[:, None, :, None, None]
            scores = jnp.where(own_rows, scores, -jnp.inf)
            block_max = round_trip(lax.optimization_barrier(jnp.max(scores, axis=(2, 4))))
            block_weight = jnp.where(own_rows, jnp.exp(scores - block_max[:, :, None, :, None]), 0.0)
            block_sum = round_trip(lax.optimization_barrier(jnp.sum(block_weight, axis=(2, 4))))
            block_out = round_trip(jnp.einsum('thpwk,pwkhn->thwn', round_trip(block_weight), prefix_values, precision=highest))
            suffix_keys, suffix_values = project_latent(latent_rows, w_ukv)
            local = jnp.einsum('thn,khn->thk', query_nope, suffix_keys.astype(jnp.float32), precision=highest)
            local = local + jnp.einsum('thr,rk->thk', query_rope, suffix_turn.astype(jnp.float32), precision=highest)
            local = local * scaling
            positions = jnp.arange(TOK_DEV, dtype=jnp.int32)
            allowed = (segment[:, None] == segment[None, :]) & (positions[None, :] <= positions[:, None])
            local = jnp.where(allowed[:, None, :], local, -jnp.inf)
            local_max = lax.optimization_barrier(jnp.max(local, axis=2))
            local_weight = jnp.where(allowed[:, None, :], jnp.exp(local - local_max[:, :, None]), 0.0)
            local_sum = lax.optimization_barrier(jnp.sum(local_weight, axis=2))
            local_out = jnp.einsum('thk,khn->thn', round_trip(local_weight), suffix_values.astype(jnp.float32), precision=highest)
            largest = jnp.maximum(local_max, lax.optimization_barrier(jnp.max(block_max, axis=2)))
            far_weight = jnp.exp(block_max - largest[:, :, None])
            near_weight = jnp.exp(local_max - largest)
            numerator = near_weight[:, :, None] * local_out + lax.optimization_barrier(jnp.sum(far_weight[:, :, :, None] * block_out, axis=2))
            denominator = near_weight * local_sum + lax.optimization_barrier(jnp.sum(far_weight * block_sum, axis=2))
            head_out = round_trip(numerator / denominator[:, :, None])
            attention = jnp.einsum('thn,hnd->td', head_out, out_heads, precision=highest)
            hidden = lax.optimization_barrier((residual_rows.astype(jnp.float32) + attention).astype(jnp.bfloat16))
            hidden_f32 = hidden.astype(jnp.float32)
            inverse = lax.rsqrt(lax.optimization_barrier(jnp.mean(hidden_f32 * hidden_f32, axis=1, keepdims=True)) + epsilon)
            normed = (hidden_f32 * inverse * gain_f32[None, :]).astype(jnp.bfloat16)
            return (hidden, normed)
        return lax.map(one_block, (query_g, latent_g, turn_g, residual_g, length_g, ident_g))
    hidden, normed = lax.map(one_group, (query_all, latent_all, turn_all, residual_all, length_all, ident_all, prefix_latent, prefix_rope))
    hidden = hidden.reshape(TOKENS, D)
    normed = normed.reshape(DEVICES, TOK_DEV, D)
    ids_dev = expert_ids.reshape(DEVICES, TOK_DEV, TOP)
    gates_dev = gate_values.reshape(DEVICES, TOK_DEV, TOP).astype(jnp.float32)
    device_rows = jnp.arange(DEVICES, dtype=jnp.int32)[:, None]

    def one_expert(running, expert):
        named = ids_dev == expert
        chosen = jnp.any(named, axis=2)
        weight = lax.optimization_barrier(jnp.sum(jnp.where(named, gates_dev, 0.0), axis=2))
        ranking = jnp.argsort(jnp.where(chosen, 0, 1).astype(jnp.int32), axis=1, stable=True)[:, :CAP].astype(jnp.int32)
        gathered = jnp.take_along_axis(normed, ranking[:, :, None], axis=1).reshape(DEVICES * CAP, D)
        picked = jnp.take_along_axis(weight, ranking, axis=1)
        output = jnp.zeros((DEVICES * CAP, D), jnp.float32)
        for half_index in range(2):
            gate_up = jnp.dot(gathered, expert_gate_up[2 * expert + half_index], preferred_element_type=jnp.float32)
            activated = (jax.nn.silu(gate_up[:, :FF_E // 2]) * gate_up[:, FF_E // 2:]).astype(jnp.bfloat16)
            output = output + round_trip(jnp.dot(activated, expert_down[2 * expert + half_index], preferred_element_type=jnp.float32))
        contribution = output.reshape(DEVICES, CAP, D) * picked[:, :, None]
        running = running.at[device_rows, ranking].add(contribution)
        return (running, None)
    mixture, unused = lax.scan(one_expert, jnp.zeros((DEVICES, TOK_DEV, D), jnp.float32), jnp.arange(EXPERTS, dtype=jnp.int32))
    return (hidden.astype(jnp.float32) + mixture.reshape(TOKENS, D)).astype(jnp.bfloat16)
```

```python
import functools

import jax
import jax.numpy as jnp
from jax import lax
from jax.experimental import pallas as pl
from jax.experimental.pallas import tpu as pltpu
from jax.sharding import PartitionSpec as P

D = 2048
HEADS = 16
NOPE = 128
ROPE = 64
LAT = 512
TOP = 6
PREF = 2
KEY = 640
STACK = 4


epsilon = 1e-06


def request_tables(lengths, request_ids, token_count):
    request_end = jnp.cumsum(lengths)
    positions = jnp.arange(token_count, dtype=jnp.int32)
    segment = jnp.sum((positions[:, None] >= request_end[None, :]).astype(jnp.int32), axis=1)
    matches = segment[:, None] == jnp.arange(request_ids.shape[0], dtype=jnp.int32)[None, :]
    prefix = jnp.sum(jnp.where(matches, request_ids[None, :], 0), axis=1)
    return (segment, prefix)


def joined_keys(latent, rope_columns):
    rope_rows = rope_columns.T
    padding = jnp.zeros((latent.shape[0], KEY - LAT - ROPE), latent.dtype)
    return jnp.concatenate([latent, rope_rows, padding], axis=1)


def contract_last(left, right):
    return lax.dot_general(
        left, right, (((1,), (1,)), ((), ())), preferred_element_type=jnp.float32
    )


def attention_kernel(
    wide_count,
    query_ref,
    rope_ref,
    own_ref,
    local_ref,
    bias_ref,
    w_ref,
    out_ref,
    keys,
    absorbed,
    send_sem,
    recv_sem,
    pass_sem,
    land_sem,
):
    me = lax.axis_index("wide")
    rows = own_ref.shape[0]
    tokens = query_ref.shape[0]
    far_rows = keys.shape[0]
    scaling = 1.0 / (NOPE + ROPE) ** 0.5
    half = wide_count // 2
    sibling = me + 1 - 2 * lax.rem(me, 2)
    slot = lambda owner: pl.ds(pl.multiple_of(owner * rows, rows), rows)

    barrier = pltpu.get_barrier_semaphore()
    peers = [sibling] + [lax.rem(me + 2 * k, wide_count) for k in range(1, half)]
    for peer in peers:
        pl.semaphore_signal(
            barrier, inc=1, device_id={"wide": peer}, device_id_type=pl.DeviceIdType.MESH
        )
    pl.semaphore_wait(barrier, half)

    first = []
    for k, peer in enumerate(peers):
        copy = pltpu.make_async_remote_copy(
            src_ref=own_ref,
            dst_ref=keys.at[slot(me)],
            send_sem=send_sem.at[k],
            recv_sem=recv_sem.at[k],
            device_id={"wide": peer},
            device_id_type=pl.DeviceIdType.MESH,
        )
        copy.start()
        first.append(copy)
    keys[slot(me), :] = own_ref[...]

    def absorb(group, carry):
        start = pl.multiple_of(group * STACK * NOPE, STACK * NOPE)
        query = query_ref[:, pl.ds(start, STACK * NOPE)]
        rope = rope_ref[:, pl.ds(start, STACK * NOPE)]
        weights = w_ref[:, pl.ds(pl.multiple_of(2 * start, 2 * STACK * NOPE), 2 * STACK * NOPE)]
        base = pl.multiple_of(group * STACK * tokens, STACK * tokens)
        for j in range(STACK):
            product = contract_last(
                query[:, j * NOPE : (j + 1) * NOPE],
                weights[:, 2 * j * NOPE : (2 * j + 1) * NOPE],
            ).astype(jnp.bfloat16)
            absorbed[pl.ds(base + j * tokens, tokens), 0:LAT] = product
            absorbed[pl.ds(base + j * tokens, tokens), LAT:KEY] = rope[
                :, j * NOPE : (j + 1) * NOPE
            ]
        return carry

    lax.fori_loop(0, HEADS // STACK, absorb, 0)

    second = []
    for k in range(1, half):
        first[k].wait_recv()
        source = lax.rem(me + wide_count - 2 * k, wide_count)
        copy = pltpu.make_async_remote_copy(
            src_ref=keys.at[slot(source)],
            dst_ref=keys.at[slot(source)],
            send_sem=pass_sem.at[k - 1],
            recv_sem=land_sem.at[k - 1],
            device_id={"wide": sibling},
            device_id_type=pl.DeviceIdType.MESH,
        )
        copy.start()
        second.append(copy)
    first[0].wait_recv()
    for copy in second:
        copy.wait_recv()

    def attend(group, carry):
        base = pl.multiple_of(group * STACK * tokens, STACK * tokens)
        query = absorbed[pl.ds(base, STACK * tokens), :]
        far = contract_last(query, keys[...]).reshape(STACK, tokens, far_rows)
        near = contract_last(query, local_ref[...]).reshape(STACK, tokens, tokens)
        far = far + bias_ref[:, 0:far_rows][None]
        near = near + bias_ref[:, far_rows:][None]
        largest = jnp.maximum(
            jnp.max(far, axis=2, keepdims=True), jnp.max(near, axis=2, keepdims=True)
        )
        far = jnp.exp((far - largest) * scaling)
        near = jnp.exp((near - largest) * scaling)
        total = jnp.sum(far, axis=2, keepdims=True) + jnp.sum(near, axis=2, keepdims=True)
        far16 = far.astype(jnp.bfloat16).reshape(STACK * tokens, far_rows)
        near16 = near.astype(jnp.bfloat16).reshape(STACK * tokens, tokens)
        mixed = jnp.dot(far16, keys[:, 0:LAT], preferred_element_type=jnp.float32)
        mixed = mixed + jnp.dot(near16, local_ref[:, 0:LAT], preferred_element_type=jnp.float32)
        mixed = (mixed / total.reshape(STACK * tokens, 1)).astype(jnp.bfloat16)
        start = pl.multiple_of(group * STACK * NOPE, STACK * NOPE)
        weights = w_ref[:, pl.ds(pl.multiple_of(2 * start, 2 * STACK * NOPE), 2 * STACK * NOPE)]
        parts = []
        for j in range(STACK):
            parts.append(
                jnp.dot(
                    mixed[j * tokens : (j + 1) * tokens],
                    weights[:, (2 * j + 1) * NOPE : (2 * j + 2) * NOPE],
                    preferred_element_type=jnp.float32,
                ).astype(jnp.bfloat16)
            )
        out_ref[:, pl.ds(start, STACK * NOPE)] = jnp.concatenate(parts, axis=1)
        return carry

    lax.fori_loop(0, HEADS // STACK, attend, 0)
    for copy in first + second:
        copy.wait_send()


def attention(queries, suffix_latent, suffix_rope, prefix_latent, prefix_rope, segment, prefix, w_ukv):
    token_count = queries.shape[0]
    wide_count = lax.axis_size("wide")
    half = wide_count // 2
    block_rows = prefix_latent.shape[2]
    rows = PREF * block_rows
    own = joined_keys(
        prefix_latent[0].reshape(rows, LAT),
        prefix_rope[0].transpose(1, 0, 2).reshape(ROPE, rows),
    )
    local = joined_keys(suffix_latent, suffix_rope)
    query_rope = queries[:, HEADS * NOPE :].reshape(token_count, HEADS, ROPE)
    query_rope = jnp.pad(query_rope, ((0, 0), (0, 0), (0, NOPE - ROPE)))
    query_rope = query_rope.reshape(token_count, HEADS * NOPE)
    positions = jnp.arange(token_count, dtype=jnp.int32)
    causal = (segment[:, None] == segment[None, :]) & (positions[None, :] <= positions[:, None])
    key_owner = jnp.tile(jnp.repeat(jnp.arange(PREF, dtype=jnp.int32), block_rows), wide_count)
    allowed = jnp.concatenate([prefix[:, None] == key_owner[None, :], causal], axis=1)
    bias = jnp.where(allowed, 0.0, -jnp.inf).astype(jnp.float32)
    vmem = pl.BlockSpec(memory_space=pltpu.VMEM)
    return pl.pallas_call(
        functools.partial(attention_kernel, wide_count),
        out_shape=jax.ShapeDtypeStruct((token_count, HEADS * NOPE), jnp.bfloat16),
        in_specs=[vmem] * 6,
        out_specs=vmem,
        scratch_shapes=[
            pltpu.VMEM((wide_count * rows, KEY), jnp.bfloat16),
            pltpu.VMEM((HEADS * token_count, KEY), jnp.bfloat16),
            pltpu.SemaphoreType.DMA((half,)),
            pltpu.SemaphoreType.DMA((half,)),
            pltpu.SemaphoreType.DMA((half - 1,)),
            pltpu.SemaphoreType.DMA((half - 1,)),
        ],
        compiler_params=pltpu.CompilerParams(
            collective_id=0, has_side_effects=True, vmem_limit_bytes=52 * 2**20
        ),
    )(queries[:, : HEADS * NOPE], query_rope, own, local, bias, w_ukv)


def expert_half(rows, gate_up_weights, down_weights):
    gate_up = jnp.dot(rows, gate_up_weights, preferred_element_type=jnp.float32)
    half_width = gate_up.shape[1] // 2
    activated = (jax.nn.silu(gate_up[:, :half_width]) * gate_up[:, half_width:]).astype(
        jnp.bfloat16
    )
    return jnp.dot(activated, down_weights, preferred_element_type=jnp.float32).astype(
        jnp.bfloat16
    )


def body(
    queries,
    suffix_latent,
    suffix_rope,
    residual,
    prefix_latent,
    prefix_rope,
    suffix_lengths,
    prefix_ids,
    w_ukv,
    w_out,
    norm_gain,
    expert_ids,
    gate_values,
    expert_gate_up,
    expert_down,
):
    token_count = queries.shape[0]
    req_count = lax.axis_size("req")
    wide_count = lax.axis_size("wide")
    devices = req_count * wide_count
    segment, prefix = request_tables(suffix_lengths[0], prefix_ids[0], token_count)
    head_out = attention(
        queries, suffix_latent, suffix_rope, prefix_latent, prefix_rope, segment, prefix, w_ukv
    )
    projected = jnp.dot(head_out, w_out, preferred_element_type=jnp.float32)
    hidden = (residual.astype(jnp.float32) + projected).astype(jnp.bfloat16)
    hidden_f32 = hidden.astype(jnp.float32)
    inverse = lax.rsqrt(jnp.mean(hidden_f32 * hidden_f32, axis=1, keepdims=True) + epsilon)
    normed = (hidden_f32 * inverse * norm_gain.astype(jnp.float32)[None, :]).astype(jnp.bfloat16)

    experts = devices // 2
    share = (token_count * TOP // experts + 2) // 2
    capacity = 2 * share
    flat_ids = expert_ids.reshape(-1)
    one_hot = (flat_ids[:, None] == jnp.arange(experts, dtype=jnp.int32)[None, :]).astype(jnp.int32)
    slot_index = jnp.sum((jnp.cumsum(one_hot, axis=0) - 1) * one_hot, axis=1)
    target = (flat_ids * capacity + slot_index).reshape(token_count, TOP)
    slots = jnp.arange(experts * capacity, dtype=jnp.int32)
    placed = [slots[:, None] == target[None, :, k] for k in range(TOP)]
    dispatch_rows = functools.reduce(jnp.logical_or, placed).astype(jnp.bfloat16)
    combine_rows = sum(
        jnp.where(placed[k], gate_values[None, :, k], 0.0) for k in range(TOP)
    )
    combine_high = combine_rows.astype(jnp.bfloat16)
    combine_low = (combine_rows - combine_high.astype(jnp.float32)).astype(jnp.bfloat16)
    outgoing = jnp.dot(dispatch_rows, normed, preferred_element_type=jnp.float32).astype(
        jnp.bfloat16
    )
    lanes = D // 128
    swap = [(i, i ^ 1) for i in range(wide_count)]

    def exchange(rows):
        moved = lax.all_to_all(
            rows.reshape(devices, share, lanes, 128),
            ("req", "wide"),
            split_axis=0,
            concat_axis=0,
            tiled=True,
        )
        return moved.reshape(devices * share, D)

    own_rows = exchange(outgoing)
    other_rows = lax.ppermute(own_rows, "wide", swap)
    own_half = expert_half(own_rows, expert_gate_up[0], expert_down[0])
    other_half = expert_half(other_rows, expert_gate_up[0], expert_down[0])
    arrived = lax.ppermute(other_half, "wide", swap)
    summed = (own_half.astype(jnp.float32) + arrived.astype(jnp.float32)).astype(jnp.bfloat16)
    returned = exchange(summed)
    both = jnp.concatenate([combine_high, combine_low], axis=1)
    mixture = lax.dot_general(
        both, returned, (((0,), (0,)), ((), ())), preferred_element_type=jnp.float32
    )
    mixture = mixture[:token_count] + mixture[token_count:]
    return (hidden_f32 + mixture).astype(jnp.bfloat16)


def solution(mesh):
    return jax.shard_map(
        body,
        mesh=mesh,
        in_specs=(
            P(("req", "wide"), None),
            P(("req", "wide"), None),
            P(None, ("req", "wide")),
            P(("req", "wide"), None),
            P("req", None, "wide", None),
            P("req", None, None, "wide"),
            P(("req", "wide"), None),
            P(("req", "wide"), None),
            P(),
            P(),
            P(),
            P(("req", "wide"), None),
            P(("req", "wide"), None),
            P(("req", "wide"), None, None),
            P(("req", "wide"), None, None),
        ),
        out_specs=P(("req", "wide"), None),
        check_vma=False,
    )
```

```python
import functools
import math

import jax
import jax.numpy as jnp
from jax import lax
from jax.experimental import pallas as pl
from jax.experimental.pallas import tpu as pltpu
from jax.sharding import PartitionSpec as P

D = 2048
HEADS = 16
NOPE = 128
ROPE = 64
LAT = 512
TOP = 6
PREF = 2
KEY = 640
STACK = 4


epsilon = 1e-06


def request_tables(lengths, request_ids, token_count):
    request_end = jnp.cumsum(lengths)
    positions = jnp.arange(token_count, dtype=jnp.int32)
    segment = jnp.sum((positions[:, None] >= request_end[None, :]).astype(jnp.int32), axis=1)
    matches = segment[:, None] == jnp.arange(request_ids.shape[0], dtype=jnp.int32)[None, :]
    prefix = jnp.sum(jnp.where(matches, request_ids[None, :], 0), axis=1)
    return (segment, prefix)


def joined_keys(latent, rope_columns):
    rope_rows = rope_columns.T
    return jnp.concatenate([latent, rope_rows, rope_rows], axis=1)


def contract_last(left, right):
    return lax.dot_general(
        left, right, (((1,), (1,)), ((), ())), preferred_element_type=jnp.float32
    )


def attention_kernel(
    wide_count,
    query_ref,
    own_ref,
    local_ref,
    bias_ref,
    w_ref,
    out_ref,
    keys,
    absorbed,
    total_out,
    total_max,
    total_sum,
    send_sem,
    recv_sem,
    pass_sem,
    land_sem,
):
    me = lax.axis_index("wide")
    rows = own_ref.shape[0]
    tokens = query_ref.shape[0]
    scaling = math.log2(math.e) / (NOPE + ROPE) ** 0.5
    half = wide_count // 2
    sibling = me + 1 - 2 * lax.rem(me, 2)
    slot = lambda place: pl.ds(place * rows, rows)

    barrier = pltpu.get_barrier_semaphore()
    peers = [sibling] + [lax.rem(me + 2 * k, wide_count) for k in range(1, half)]
    for peer in peers:
        pl.semaphore_signal(
            barrier, inc=1, device_id={"wide": peer}, device_id_type=pl.DeviceIdType.MESH
        )
    pl.semaphore_wait(barrier, half)

    first = []
    for k, peer in enumerate(peers):
        copy = pltpu.make_async_remote_copy(
            src_ref=own_ref,
            dst_ref=keys.at[slot(2 * k if k else 1)],
            send_sem=send_sem.at[k],
            recv_sem=recv_sem.at[k],
            device_id={"wide": peer},
            device_id_type=pl.DeviceIdType.MESH,
        )
        copy.start()
        first.append(copy)
    keys[slot(0), :] = own_ref[...]
    low = lax.broadcasted_iota(jnp.int32, (tokens, NOPE), 1) < ROPE

    def group_weights(group):
        width = 2 * STACK * NOPE
        return w_ref[:, pl.ds(pl.multiple_of(group * width, width), width)]

    def absorb(group, carry):
        query = query_ref[:, pl.ds(pl.multiple_of(group * STACK * NOPE, NOPE), STACK * NOPE)]
        rope_start = pl.multiple_of(HEADS * NOPE + group * STACK * ROPE, NOPE)
        rope = query_ref[:, pl.ds(rope_start, STACK * ROPE)].astype(jnp.float32) * scaling
        weights = group_weights(group)
        base = pl.multiple_of(group * STACK * tokens, STACK * tokens)
        for j in range(STACK):
            product = contract_last(
                query[:, j * NOPE : (j + 1) * NOPE],
                weights[:, 2 * j * NOPE : (2 * j + 1) * NOPE],
            )
            pair = rope[:, j // 2 * NOPE : (j // 2 + 1) * NOPE]
            pair = jnp.where(low, pair, 0.0) if j % 2 == 0 else jnp.where(low, 0.0, pair)
            place = pl.ds(base + j * tokens, tokens)
            absorbed[place, 0:LAT] = (product * scaling).astype(jnp.bfloat16)
            absorbed[place, LAT:KEY] = pair.astype(jnp.bfloat16)
        return carry

    lax.fori_loop(0, HEADS // STACK, absorb, 0)

    def scores(query, begin, blocks):
        found = contract_last(query, keys[begin * rows : (begin + blocks) * rows, :])
        found = found.reshape(STACK, tokens, blocks * rows)
        bias = jnp.concatenate([bias_ref[:, 0:rows]] * blocks, axis=1)
        return found + bias[None]

    def flat(values):
        return values.reshape(STACK * tokens, values.shape[2])

    first[0].wait_recv()

    def attend_near(group, carry):
        place = pl.ds(pl.multiple_of(group * STACK * tokens, STACK * tokens), STACK * tokens)
        query = absorbed[place, :]
        far = scores(query, 0, 2)
        near = contract_last(query, local_ref[...]).reshape(STACK, tokens, tokens)
        near = near + bias_ref[:, rows:][None]
        largest = jnp.maximum(
            jnp.max(far, axis=2, keepdims=True), jnp.max(near, axis=2, keepdims=True)
        )
        far = jnp.exp2(far - largest)
        near = jnp.exp2(near - largest)
        total_max[place, :] = flat(largest)
        total_sum[place, :] = flat(
            jnp.sum(far, axis=2, keepdims=True) + jnp.sum(near, axis=2, keepdims=True)
        )
        total_out[place, :] = jnp.dot(
            flat(far).astype(jnp.bfloat16),
            keys[0 : 2 * rows, 0:LAT],
            preferred_element_type=jnp.float32,
        ) + jnp.dot(
            flat(near).astype(jnp.bfloat16),
            local_ref[:, 0:LAT],
            preferred_element_type=jnp.float32,
        )
        return carry

    lax.fori_loop(0, HEADS // STACK, attend_near, 0)

    second = []
    for k in range(1, half):
        first[k].wait_recv()
        copy = pltpu.make_async_remote_copy(
            src_ref=keys.at[slot(2 * k)],
            dst_ref=keys.at[slot(2 * k + 1)],
            send_sem=pass_sem.at[k - 1],
            recv_sem=land_sem.at[k - 1],
            device_id={"wide": sibling},
            device_id_type=pl.DeviceIdType.MESH,
        )
        copy.start()
        second.append(copy)
    for copy in second:
        copy.wait_recv()

    def attend(group, carry):
        place = pl.ds(pl.multiple_of(group * STACK * tokens, STACK * tokens), STACK * tokens)
        far = scores(absorbed[place, :], 2, wide_count - 2)
        before = total_max[place, :].reshape(STACK, tokens, 1)
        largest = jnp.maximum(jnp.max(far, axis=2, keepdims=True), before)
        far = jnp.exp2(far - largest)
        keep = flat(jnp.exp2(before - largest))
        total = keep * total_sum[place, :] + flat(jnp.sum(far, axis=2, keepdims=True))
        mixed = keep * total_out[place, :] + jnp.dot(
            flat(far).astype(jnp.bfloat16),
            keys[2 * rows :, 0:LAT],
            preferred_element_type=jnp.float32,
        )
        mixed = (mixed / total).astype(jnp.bfloat16)
        weights = group_weights(group)
        parts = []
        for j in range(STACK):
            parts.append(
                jnp.dot(
                    mixed[j * tokens : (j + 1) * tokens],
                    weights[:, (2 * j + 1) * NOPE : (2 * j + 2) * NOPE],
                    preferred_element_type=jnp.float32,
                ).astype(jnp.bfloat16)
            )
        start = pl.multiple_of(group * STACK * NOPE, STACK * NOPE)
        out_ref[:, pl.ds(start, STACK * NOPE)] = jnp.concatenate(parts, axis=1)
        return carry

    lax.fori_loop(0, HEADS // STACK, attend, 0)
    for copy in first + second:
        copy.wait_send()


def attention(queries, suffix_latent, suffix_rope, prefix_latent, prefix_rope, segment, prefix, w_ukv):
    token_count = queries.shape[0]
    wide_count = lax.axis_size("wide")
    half = wide_count // 2
    block_rows = prefix_latent.shape[2]
    rows = PREF * block_rows
    own = joined_keys(
        prefix_latent[0].reshape(rows, LAT),
        prefix_rope[0].transpose(1, 0, 2).reshape(ROPE, rows),
    )
    local = joined_keys(suffix_latent, suffix_rope)
    positions = jnp.arange(token_count, dtype=jnp.int32)
    causal = (segment[:, None] == segment[None, :]) & (positions[None, :] <= positions[:, None])
    key_owner = jnp.repeat(jnp.arange(PREF, dtype=jnp.int32), block_rows)
    allowed = jnp.concatenate([prefix[:, None] == key_owner[None, :], causal], axis=1)
    bias = jnp.where(allowed, 0.0, -jnp.inf).astype(jnp.float32)
    vmem = pl.BlockSpec(memory_space=pltpu.VMEM)
    stacked = HEADS * token_count
    return pl.pallas_call(
        functools.partial(attention_kernel, wide_count),
        out_shape=jax.ShapeDtypeStruct((token_count, HEADS * NOPE), jnp.bfloat16),
        in_specs=[vmem] * 5,
        out_specs=vmem,
        scratch_shapes=[
            pltpu.VMEM((wide_count * rows, KEY), jnp.bfloat16),
            pltpu.VMEM((stacked, KEY), jnp.bfloat16),
            pltpu.VMEM((stacked, LAT), jnp.float32),
            pltpu.VMEM((stacked, 1), jnp.float32),
            pltpu.VMEM((stacked, 1), jnp.float32),
            pltpu.SemaphoreType.DMA((half,)),
            pltpu.SemaphoreType.DMA((half,)),
            pltpu.SemaphoreType.DMA((half - 1,)),
            pltpu.SemaphoreType.DMA((half - 1,)),
        ],
        compiler_params=pltpu.CompilerParams(
            collective_id=0, has_side_effects=True, vmem_limit_bytes=56 * 2**20
        ),
    )(queries, own, local, bias, w_ukv)


def expert_half(rows, gate_up_weights, down_weights):
    gate_up = jnp.dot(rows, gate_up_weights, preferred_element_type=jnp.float32)
    half_width = gate_up.shape[1] // 2
    activated = (jax.nn.silu(gate_up[:, :half_width]) * gate_up[:, half_width:]).astype(
        jnp.bfloat16
    )
    return jnp.dot(activated, down_weights, preferred_element_type=jnp.float32).astype(
        jnp.bfloat16
    )


def body(
    queries,
    suffix_latent,
    suffix_rope,
    residual,
    prefix_latent,
    prefix_rope,
    suffix_lengths,
    prefix_ids,
    w_ukv,
    w_out,
    norm_gain,
    expert_ids,
    gate_values,
    expert_gate_up,
    expert_down,
):
    token_count = queries.shape[0]
    req_count = lax.axis_size("req")
    wide_count = lax.axis_size("wide")
    devices = req_count * wide_count
    segment, prefix = request_tables(suffix_lengths[0], prefix_ids[0], token_count)
    head_out = attention(
        queries, suffix_latent, suffix_rope, prefix_latent, prefix_rope, segment, prefix, w_ukv
    )
    projected = jnp.dot(head_out, w_out, preferred_element_type=jnp.float32)
    hidden = (residual.astype(jnp.float32) + projected).astype(jnp.bfloat16)
    hidden_f32 = hidden.astype(jnp.float32)
    inverse = lax.rsqrt(jnp.mean(hidden_f32 * hidden_f32, axis=1, keepdims=True) + epsilon)
    normed = (hidden_f32 * inverse * norm_gain.astype(jnp.float32)[None, :]).astype(jnp.bfloat16)

    experts = devices // 2
    share = (token_count * TOP // experts + 2) // 2
    capacity = 2 * share
    flat_ids = expert_ids.reshape(-1)
    one_hot = (flat_ids[:, None] == jnp.arange(experts, dtype=jnp.int32)[None, :]).astype(jnp.int32)
    slot_index = jnp.sum((jnp.cumsum(one_hot, axis=0) - 1) * one_hot, axis=1)
    target = (flat_ids * capacity + slot_index).reshape(token_count, TOP)
    slots = jnp.arange(experts * capacity, dtype=jnp.int32)
    placed = [slots[:, None] == target[None, :, k] for k in range(TOP)]
    dispatch_rows = functools.reduce(jnp.logical_or, placed).astype(jnp.bfloat16)
    combine_rows = sum(
        jnp.where(placed[k], gate_values[None, :, k], 0.0) for k in range(TOP)
    )
    combine_high = combine_rows.astype(jnp.bfloat16)
    combine_low = (combine_rows - combine_high.astype(jnp.float32)).astype(jnp.bfloat16)
    outgoing = jnp.dot(dispatch_rows, normed, preferred_element_type=jnp.float32).astype(
        jnp.bfloat16
    )
    lanes = D // 128
    swap = [(i, i ^ 1) for i in range(wide_count)]

    def exchange(rows):
        moved = lax.all_to_all(
            rows.reshape(devices, share, lanes, 128),
            ("req", "wide"),
            split_axis=0,
            concat_axis=0,
            tiled=True,
        )
        return moved.reshape(devices * share, D)

    own_rows = exchange(outgoing)
    other_rows = lax.ppermute(own_rows, "wide", swap)
    own_half = expert_half(own_rows, expert_gate_up[0], expert_down[0])
    other_half = expert_half(other_rows, expert_gate_up[0], expert_down[0])
    arrived = lax.ppermute(other_half, "wide", swap)
    summed = (own_half.astype(jnp.float32) + arrived.astype(jnp.float32)).astype(jnp.bfloat16)
    returned = exchange(summed)
    both = jnp.concatenate([combine_high, combine_low], axis=1)
    mixture = lax.dot_general(
        both, returned, (((0,), (0,)), ((), ())), preferred_element_type=jnp.float32
    )
    mixture = mixture[:token_count] + mixture[token_count:]
    return (hidden_f32 + mixture).astype(jnp.bfloat16)


def solution(mesh):
    return jax.shard_map(
        body,
        mesh=mesh,
        in_specs=(
            P(("req", "wide"), None),
            P(("req", "wide"), None),
            P(None, ("req", "wide")),
            P(("req", "wide"), None),
            P("req", None, "wide", None),
            P("req", None, None, "wide"),
            P(("req", "wide"), None),
            P(("req", "wide"), None),
            P(),
            P(),
            P(),
            P(("req", "wide"), None),
            P(("req", "wide"), None),
            P(("req", "wide"), None, None),
            P(("req", "wide"), None, None),
        ),
        out_specs=P(("req", "wide"), None),
        check_vma=False,
    )
```

```python
import functools
import math

import jax
import jax.numpy as jnp
from jax import lax
from jax.experimental import pallas as pl
from jax.experimental.pallas import tpu as pltpu
from jax.sharding import PartitionSpec as P

D = 2048
HEADS = 16
NOPE = 128
ROPE = 64
LAT = 512
TOP = 6
PREF = 2
KEY = 640
STACK = 4


epsilon = 1e-06


def request_tables(lengths, request_ids, token_count):
    request_end = jnp.cumsum(lengths)
    positions = jnp.arange(token_count, dtype=jnp.int32)
    segment = jnp.sum((positions[:, None] >= request_end[None, :]).astype(jnp.int32), axis=1)
    matches = segment[:, None] == jnp.arange(request_ids.shape[0], dtype=jnp.int32)[None, :]
    prefix = jnp.sum(jnp.where(matches, request_ids[None, :], 0), axis=1)
    return (segment, prefix)


def joined_keys(latent, rope_columns):
    rope_rows = rope_columns.T
    return jnp.concatenate([latent, rope_rows, rope_rows], axis=1)


def contract_last(left, right):
    return lax.dot_general(
        left, right, (((1,), (1,)), ((), ())), preferred_element_type=jnp.float32
    )


def attention_kernel(
    wide_count,
    query_ref,
    own_ref,
    local_ref,
    bias_ref,
    w_ref,
    out_ref,
    keys,
    absorbed,
    total_out,
    total_max,
    total_sum,
    send_sem,
    recv_sem,
    pass_sem,
    land_sem,
):
    me = lax.axis_index("wide")
    rows = own_ref.shape[0]
    tokens = query_ref.shape[0]
    scaling = math.log2(math.e) / (NOPE + ROPE) ** 0.5
    half = wide_count // 2
    sibling = me + 1 - 2 * lax.rem(me, 2)
    slot = lambda place: pl.ds(place * rows, rows)

    barrier = pltpu.get_barrier_semaphore()
    peers = [sibling] + [lax.rem(me + 2 * k, wide_count) for k in range(1, half)]
    for peer in peers:
        pl.semaphore_signal(
            barrier, inc=1, device_id={"wide": peer}, device_id_type=pl.DeviceIdType.MESH
        )
    pl.semaphore_wait(barrier, half)

    first = []
    for k, peer in enumerate(peers):
        copy = pltpu.make_async_remote_copy(
            src_ref=own_ref,
            dst_ref=keys.at[slot(2 * k if k else 1)],
            send_sem=send_sem.at[k],
            recv_sem=recv_sem.at[k],
            device_id={"wide": peer},
            device_id_type=pl.DeviceIdType.MESH,
        )
        copy.start()
        first.append(copy)
    keys[slot(0), :] = own_ref[...]
    low = lax.broadcasted_iota(jnp.int32, (tokens, NOPE), 1) < ROPE

    def group_weights(group):
        width = 2 * STACK * NOPE
        return w_ref[:, pl.ds(pl.multiple_of(group * width, width), width)]

    def absorb(group, carry):
        query = query_ref[:, pl.ds(pl.multiple_of(group * STACK * NOPE, NOPE), STACK * NOPE)]
        rope_start = pl.multiple_of(HEADS * NOPE + group * STACK * ROPE, NOPE)
        rope = query_ref[:, pl.ds(rope_start, STACK * ROPE)].astype(jnp.float32) * scaling
        weights = group_weights(group)
        base = pl.multiple_of(group * STACK * tokens, STACK * tokens)
        for j in range(STACK):
            product = contract_last(
                query[:, j * NOPE : (j + 1) * NOPE],
                weights[:, 2 * j * NOPE : (2 * j + 1) * NOPE],
            )
            pair = rope[:, j // 2 * NOPE : (j // 2 + 1) * NOPE]
            pair = jnp.where(low, pair, 0.0) if j % 2 == 0 else jnp.where(low, 0.0, pair)
            place = pl.ds(base + j * tokens, tokens)
            absorbed[place, 0:LAT] = (product * scaling).astype(jnp.bfloat16)
            absorbed[place, LAT:KEY] = pair.astype(jnp.bfloat16)
        return carry

    lax.fori_loop(0, HEADS // STACK, absorb, 0)

    def scores(query, begin, blocks):
        found = contract_last(query, keys[begin * rows : (begin + blocks) * rows, :])
        found = found.reshape(STACK, tokens, blocks * rows)
        bias = jnp.concatenate([bias_ref[:, 0:rows]] * blocks, axis=1)
        return found + bias[None]

    def flat(values):
        return values.reshape(STACK * tokens, values.shape[2])

    first[0].wait_recv()

    def attend_near(group, carry):
        place = pl.ds(pl.multiple_of(group * STACK * tokens, STACK * tokens), STACK * tokens)
        query = absorbed[place, :]
        far = scores(query, 0, 2)
        near = contract_last(query, local_ref[...]).reshape(STACK, tokens, tokens)
        near = near + bias_ref[:, rows:][None]
        largest = jnp.maximum(
            jnp.max(far, axis=2, keepdims=True), jnp.max(near, axis=2, keepdims=True)
        )
        far = jnp.exp2(far - largest)
        near = jnp.exp2(near - largest)
        total_max[place, :] = flat(largest)
        total_sum[place, :] = flat(
            jnp.sum(far, axis=2, keepdims=True) + jnp.sum(near, axis=2, keepdims=True)
        )
        total_out[place, :] = jnp.dot(
            flat(far).astype(jnp.bfloat16),
            keys[0 : 2 * rows, 0:LAT],
            preferred_element_type=jnp.float32,
        ) + jnp.dot(
            flat(near).astype(jnp.bfloat16),
            local_ref[:, 0:LAT],
            preferred_element_type=jnp.float32,
        )
        return carry

    lax.fori_loop(0, HEADS // STACK, attend_near, 0)

    second = []
    for k in range(1, half):
        first[k].wait_recv()
        copy = pltpu.make_async_remote_copy(
            src_ref=keys.at[slot(2 * k)],
            dst_ref=keys.at[slot(2 * k + 1)],
            send_sem=pass_sem.at[k - 1],
            recv_sem=land_sem.at[k - 1],
            device_id={"wide": sibling},
            device_id_type=pl.DeviceIdType.MESH,
        )
        copy.start()
        second.append(copy)
    for copy in second:
        copy.wait_recv()

    def attend(group, carry):
        place = pl.ds(pl.multiple_of(group * STACK * tokens, STACK * tokens), STACK * tokens)
        far = scores(absorbed[place, :], 2, wide_count - 2)
        before = total_max[place, :].reshape(STACK, tokens, 1)
        largest = jnp.maximum(jnp.max(far, axis=2, keepdims=True), before)
        far = jnp.exp2(far - largest)
        keep = flat(jnp.exp2(before - largest))
        total = keep * total_sum[place, :] + flat(jnp.sum(far, axis=2, keepdims=True))
        mixed = keep * total_out[place, :] + jnp.dot(
            flat(far).astype(jnp.bfloat16),
            keys[2 * rows :, 0:LAT],
            preferred_element_type=jnp.float32,
        )
        mixed = (mixed / total).astype(jnp.bfloat16)
        weights = group_weights(group)
        parts = []
        for j in range(STACK):
            parts.append(
                jnp.dot(
                    mixed[j * tokens : (j + 1) * tokens],
                    weights[:, (2 * j + 1) * NOPE : (2 * j + 2) * NOPE],
                    preferred_element_type=jnp.float32,
                ).astype(jnp.bfloat16)
            )
        start = pl.multiple_of(group * STACK * NOPE, STACK * NOPE)
        out_ref[:, pl.ds(start, STACK * NOPE)] = jnp.concatenate(parts, axis=1)
        return carry

    lax.fori_loop(0, HEADS // STACK, attend, 0)
    for copy in first + second:
        copy.wait_send()


def attention(queries, suffix_latent, suffix_rope, prefix_latent, prefix_rope, segment, prefix, w_ukv):
    token_count = queries.shape[0]
    wide_count = lax.axis_size("wide")
    half = wide_count // 2
    block_rows = prefix_latent.shape[2]
    rows = PREF * block_rows
    own = joined_keys(
        prefix_latent[0].reshape(rows, LAT),
        prefix_rope[0].transpose(1, 0, 2).reshape(ROPE, rows),
    )
    local = joined_keys(suffix_latent, suffix_rope)
    positions = jnp.arange(token_count, dtype=jnp.int32)
    causal = (segment[:, None] == segment[None, :]) & (positions[None, :] <= positions[:, None])
    key_owner = jnp.repeat(jnp.arange(PREF, dtype=jnp.int32), block_rows)
    allowed = jnp.concatenate([prefix[:, None] == key_owner[None, :], causal], axis=1)
    bias = jnp.where(allowed, 0.0, -jnp.inf).astype(jnp.float32)
    vmem = pl.BlockSpec(memory_space=pltpu.VMEM)
    stacked = HEADS * token_count
    return pl.pallas_call(
        functools.partial(attention_kernel, wide_count),
        out_shape=jax.ShapeDtypeStruct((token_count, HEADS * NOPE), jnp.bfloat16),
        in_specs=[vmem] * 5,
        out_specs=vmem,
        scratch_shapes=[
            pltpu.VMEM((wide_count * rows, KEY), jnp.bfloat16),
            pltpu.VMEM((stacked, KEY), jnp.bfloat16),
            pltpu.VMEM((stacked, LAT), jnp.float32),
            pltpu.VMEM((stacked, 1), jnp.float32),
            pltpu.VMEM((stacked, 1), jnp.float32),
            pltpu.SemaphoreType.DMA((half,)),
            pltpu.SemaphoreType.DMA((half,)),
            pltpu.SemaphoreType.DMA((half - 1,)),
            pltpu.SemaphoreType.DMA((half - 1,)),
        ],
        compiler_params=pltpu.CompilerParams(
            collective_id=0, has_side_effects=True, vmem_limit_bytes=56 * 2**20
        ),
    )(queries, own, local, bias, w_ukv)


def mesh_peers():
    me_req, me_wide = lax.axis_index("req"), lax.axis_index("wide")
    req_count, wide_count = lax.axis_size("req"), lax.axis_size("wide")
    above = [lax.rem(me_req + k, req_count) for k in range(req_count)]
    beside = [lax.rem(me_wide + j, wide_count) for j in range(wide_count)]
    return above, beside


def greet(above, beside):
    barrier = pltpu.get_barrier_semaphore()
    for peer in above[1:]:
        pl.semaphore_signal(
            barrier, inc=1, device_id={"req": peer}, device_id_type=pl.DeviceIdType.MESH
        )
    for peer in beside[1:]:
        pl.semaphore_signal(
            barrier, inc=1, device_id={"wide": peer}, device_id_type=pl.DeviceIdType.MESH
        )
    pl.semaphore_wait(barrier, len(above) + len(beside) - 2)


def send(src, dst, send_sem, recv_sem, target):
    copy = pltpu.make_async_remote_copy(
        src_ref=src,
        dst_ref=dst,
        send_sem=send_sem,
        recv_sem=recv_sem,
        device_id=target,
        device_id_type=pl.DeviceIdType.MESH,
    )
    copy.start()
    return copy


def dispatch_kernel(
    share,
    normed_ref,
    select_ref,
    out_ref,
    tokens,
    selects,
    picked,
    token_sems,
    select_sems,
    row_send,
    row_recv,
    own_sem,
):
    above, beside = mesh_peers()
    greet(above, beside)
    layer_rows = picked.shape[1]
    layer = lambda r: pl.ds(pl.multiple_of(r * layer_rows, layer_rows), layer_rows)
    piece = lambda w: pl.ds(pl.multiple_of(w * share, share), share)
    sent, asked, moved, kept = [None], [None], [], []
    for k in range(1, len(above)):
        target = {"req": above[k]}
        asked.append(
            send(
                select_ref.at[layer(above[k])],
                selects.at[k - 1],
                select_sems.at[0, k - 1],
                select_sems.at[1, k - 1],
                target,
            )
        )
        sent.append(
            send(
                normed_ref,
                tokens.at[k - 1],
                token_sems.at[0, k - 1],
                token_sems.at[1, k - 1],
                target,
            )
        )
    for k in range(len(above)):
        if k == 0:
            block, choice = normed_ref[...], select_ref[layer(above[0]), :]
        else:
            asked[k].wait_recv()
            sent[k].wait_recv()
            block, choice = tokens[k - 1], selects[k - 1]
        picked[k] = jnp.dot(choice, block, preferred_element_type=jnp.float32).astype(jnp.bfloat16)
        for j in range(1, len(beside)):
            moved.append(
                send(
                    picked.at[k, piece(beside[j])],
                    out_ref.at[k, j],
                    row_send.at[k, j - 1],
                    row_recv.at[k, j - 1],
                    {"wide": beside[j]},
                )
            )
        copy = pltpu.make_async_copy(
            picked.at[k, piece(beside[0])], out_ref.at[k, 0], own_sem.at[k]
        )
        copy.start()
        kept.append(copy)
    for copy in moved:
        copy.wait()
    for copy in kept:
        copy.wait()
    for copy in asked[1:] + sent[1:]:
        copy.wait_send()


def combine_kernel(
    share,
    rows_ref,
    gate_ref,
    hidden_ref,
    out_ref,
    gates,
    held,
    partial,
    arrived,
    gate_sems,
    row_send,
    row_recv,
    own_sem,
    part_sems,
):
    above, beside = mesh_peers()
    greet(above, beside)
    layers, places = len(above), len(beside)
    layer_rows = held.shape[1]
    layer = lambda r: pl.ds(pl.multiple_of(r * layer_rows, layer_rows), layer_rows)
    mine = pl.ds(pl.multiple_of(beside[0] * share, share), share)
    order = list(range(1, layers)) + [0]
    given = [None] + [
        send(
            gate_ref.at[layer(above[k])],
            gates.at[k - 1],
            gate_sems.at[0, k - 1],
            gate_sems.at[1, k - 1],
            {"req": above[k]},
        )
        for k in range(1, layers)
    ]
    moved, kept = {}, {}
    for k in order:
        for j in range(1, places):
            moved[k, j] = send(
                rows_ref.at[k, j],
                held.at[k, mine],
                row_send.at[k, j - 1],
                row_recv.at[k, j - 1],
                {"wide": beside[places - j]},
            )
        kept[k] = pltpu.make_async_copy(rows_ref.at[k, 0], held.at[k, mine], own_sem.at[k])
        kept[k].start()
    parts = []
    total = None
    for k in order:
        for j in range(1, places):
            moved[k, j].wait_recv()
        kept[k].wait()
        if k:
            given[k].wait_recv()
            weights = gates[k - 1]
        else:
            weights = gate_ref[layer(above[0]), :]
        mixed = lax.dot_general(
            weights, held[k], (((0,), (0,)), ((), ())), preferred_element_type=jnp.float32
        )
        if k:
            partial[k - 1] = mixed.astype(jnp.bfloat16)
            parts.append(
                send(
                    partial.at[k - 1],
                    arrived.at[k - 1],
                    part_sems.at[0, k - 1],
                    part_sems.at[1, k - 1],
                    {"req": above[layers - k]},
                )
            )
        else:
            total = mixed + hidden_ref[...].astype(jnp.float32)
    for k, copy in enumerate(parts):
        copy.wait_recv()
        total = total + arrived[k].astype(jnp.float32)
    out_ref[...] = total.astype(jnp.bfloat16)
    for copy in given[1:] + list(moved.values()) + parts:
        copy.wait_send()


def dispatch(normed, select, share):
    req_count, wide_count = lax.axis_size("req"), lax.axis_size("wide")
    token_count = normed.shape[0]
    vmem = pl.BlockSpec(memory_space=pltpu.VMEM)
    dma = pltpu.SemaphoreType.DMA
    return pl.pallas_call(
        functools.partial(dispatch_kernel, share),
        out_shape=jax.ShapeDtypeStruct((req_count, wide_count, share, D), jnp.bfloat16),
        in_specs=[vmem, vmem],
        out_specs=pl.BlockSpec(memory_space=pl.ANY),
        scratch_shapes=[
            pltpu.VMEM((req_count - 1, token_count, D), jnp.bfloat16),
            pltpu.VMEM((req_count - 1, wide_count * share, token_count), jnp.bfloat16),
            pltpu.VMEM((req_count, wide_count * share, D), jnp.bfloat16),
            dma((2, req_count - 1)),
            dma((2, req_count - 1)),
            dma((req_count, wide_count - 1)),
            dma((req_count, wide_count - 1)),
            dma((req_count,)),
        ],
        compiler_params=pltpu.CompilerParams(
            collective_id=1, has_side_effects=True, vmem_limit_bytes=48 * 2**20
        ),
    )(normed, select)


def combine(rows, gates, hidden, share):
    req_count, wide_count = lax.axis_size("req"), lax.axis_size("wide")
    token_count = hidden.shape[0]
    vmem = pl.BlockSpec(memory_space=pltpu.VMEM)
    dma = pltpu.SemaphoreType.DMA
    return pl.pallas_call(
        functools.partial(combine_kernel, share),
        out_shape=jax.ShapeDtypeStruct((token_count, D), jnp.bfloat16),
        in_specs=[pl.BlockSpec(memory_space=pl.ANY), vmem, vmem],
        out_specs=vmem,
        scratch_shapes=[
            pltpu.VMEM((req_count - 1, wide_count * share, token_count), jnp.bfloat16),
            pltpu.VMEM((req_count, wide_count * share, D), jnp.bfloat16),
            pltpu.VMEM((req_count - 1, token_count, D), jnp.bfloat16),
            pltpu.VMEM((req_count - 1, token_count, D), jnp.bfloat16),
            dma((2, req_count - 1)),
            dma((req_count, wide_count - 1)),
            dma((req_count, wide_count - 1)),
            dma((req_count,)),
            dma((2, req_count - 1)),
        ],
        compiler_params=pltpu.CompilerParams(
            collective_id=2, has_side_effects=True, vmem_limit_bytes=48 * 2**20
        ),
    )(rows, gates, hidden)


def expert_half(rows, gate_up_weights, down_weights):
    gate_up = jnp.dot(rows, gate_up_weights, preferred_element_type=jnp.float32)
    half_width = gate_up.shape[1] // 2
    activated = (jax.nn.silu(gate_up[:, :half_width]) * gate_up[:, half_width:]).astype(
        jnp.bfloat16
    )
    return jnp.dot(activated, down_weights, preferred_element_type=jnp.float32).astype(
        jnp.bfloat16
    )


def body(
    queries,
    suffix_latent,
    suffix_rope,
    residual,
    prefix_latent,
    prefix_rope,
    suffix_lengths,
    prefix_ids,
    w_ukv,
    w_out,
    norm_gain,
    expert_ids,
    gate_values,
    expert_gate_up,
    expert_down,
):
    token_count = queries.shape[0]
    req_count = lax.axis_size("req")
    wide_count = lax.axis_size("wide")
    devices = req_count * wide_count
    segment, prefix = request_tables(suffix_lengths[0], prefix_ids[0], token_count)
    head_out = attention(
        queries, suffix_latent, suffix_rope, prefix_latent, prefix_rope, segment, prefix, w_ukv
    )
    projected = jnp.dot(head_out, w_out, preferred_element_type=jnp.float32)
    hidden = (residual.astype(jnp.float32) + projected).astype(jnp.bfloat16)
    hidden_f32 = hidden.astype(jnp.float32)
    inverse = lax.rsqrt(jnp.mean(hidden_f32 * hidden_f32, axis=1, keepdims=True) + epsilon)
    normed = (hidden_f32 * inverse * norm_gain.astype(jnp.float32)[None, :]).astype(jnp.bfloat16)

    experts = devices // 2
    used = (token_count * TOP // experts + 2) // 2
    share = (used + 15) // 16 * 16
    flat_ids = expert_ids.reshape(-1)
    one_hot = (flat_ids[:, None] == jnp.arange(experts, dtype=jnp.int32)[None, :]).astype(jnp.int32)
    slot_index = jnp.sum((jnp.cumsum(one_hot, axis=0) - 1) * one_hot, axis=1)
    second = (slot_index >= used).astype(jnp.int32)
    target = (2 * flat_ids + second) * share + slot_index - second * used
    target = target.reshape(token_count, TOP)
    slots = jnp.arange(devices * share, dtype=jnp.int32)
    placed = [slots[:, None] == target[None, :, k] for k in range(TOP)]
    select = functools.reduce(jnp.logical_or, placed).astype(jnp.bfloat16)
    gates = sum(jnp.where(placed[k], gate_values[None, :, k], 0.0) for k in range(TOP))
    gates = gates.astype(jnp.bfloat16)
    swap = [(i, i ^ 1) for i in range(wide_count)]
    own_rows = dispatch(normed, select, share).reshape(devices * share, D)
    other_rows = lax.ppermute(own_rows, "wide", swap)
    other_half = expert_half(other_rows, expert_gate_up[0], expert_down[0])
    arrived = lax.ppermute(other_half, "wide", swap)
    own_half = expert_half(own_rows, expert_gate_up[0], expert_down[0])
    summed = (own_half.astype(jnp.float32) + arrived.astype(jnp.float32)).astype(jnp.bfloat16)
    return combine(summed.reshape(req_count, wide_count, share, D), gates, hidden, share)


def solution(mesh):
    return jax.shard_map(
        body,
        mesh=mesh,
        in_specs=(
            P(("req", "wide"), None),
            P(("req", "wide"), None),
            P(None, ("req", "wide")),
            P(("req", "wide"), None),
            P("req", None, "wide", None),
            P("req", None, None, "wide"),
            P(("req", "wide"), None),
            P(("req", "wide"), None),
            P(),
            P(),
            P(),
            P(("req", "wide"), None),
            P(("req", "wide"), None),
            P(("req", "wide"), None, None),
            P(("req", "wide"), None, None),
        ),
        out_specs=P(("req", "wide"), None),
        check_vma=False,
    )
```
